512 devices in a mesh: users: 32 (over y, x, core), items: 16 (over z).
Axes of the slice: x: 4, y: 4, z: 16, core: 2. Of those that a mesh axis runs over, the one named last changes fastest.
Arguments:
- user_emb: bfloat16 [65536, 256], P('users'), may hold values from -0.375 to 0.375
- samples: int32 [512, 64], P('users'), may hold values from 0 to 127, as said below
- pos_item: int32 [65536], P('users'), may hold values from 0 to 16383
- item_feat: bfloat16 [16384, 1024], P(('items', 'users')), may hold values from -0.1875 to 0.1875
- tower_w: bfloat16 [1024, 256], replicated, may hold values from -5 to 5
- item_bias: bfloat16 [16384], P(('items', 'users')), may hold values from -4 to 352
Outputs:
- user_loss: float32 [65536], P('users')
- user_grad: float32 [65536, 256], P(('users', 'items'))
- weight_grad: float32 [1024, 256], replicated
The draws below stay inside these ranges and needn't reach their ends.
Inputs may be any that keep to these rules, and one draw needn't show every extreme that they name: `samples`: each row lists 64 distinct cluster ids. Clusters k * 8 to (k + 1) * 8 - 1 form item shard k; at most 8 ids of one row fall in any one shard, and in every row some shard holds exactly 8 of them.
All inputs are finite; a program needn't handle non-finite values.
Results may differ from the reference program's by a relative error of at most 0.0036.
Values may be sent and summed in bfloat16 or wider, within the bound.
No kernel may reach another device: no remote copies, remote signals or barrier semaphores. Data moves between devices by JAX's collectives and lax.ppermute only.
A program may use at most 64 MiB of HBM per device.

```python
import jax
import jax.numpy as jnp
from jax import lax

F = 1024
DE = 256
CL = 128
BU = 128
SHARD_CLUS = 8
MOST = 8
SAMPLES = 64
ITEMS = 16384
CLUSTERS = 128
BLOCKS = 512
USERS = 65536


def draw_samples(key, part):
    shard_total = CLUSTERS // SHARD_CLUS
    half_total = shard_total // 2

    def one_block(block_key):
        key_order, key_split, key_rank, key_shuffle = jax.random.split(block_key, 4)
        order = jax.random.permutation(key_order, shard_total)
        split_at = jax.random.randint(key_split, (half_total,), 0, MOST + 1)
        split_at = split_at.at[0].set(0)
        pair_counts = jnp.stack([MOST - split_at, split_at], axis=1).reshape(shard_total)
        counts = jnp.zeros((shard_total,), jnp.int32).at[order].set(pair_counts.astype(jnp.int32))
        rank_keys = jax.random.split(key_rank, shard_total)
        ranks = jax.vmap(lambda rank_key: jax.random.permutation(rank_key, SHARD_CLUS))(rank_keys)
        chosen = (ranks < counts[:, None]).reshape(CLUSTERS)
        cluster_ids = jnp.arange(CLUSTERS, dtype=jnp.int32)
        order_score = jnp.where(chosen, 0, 1).astype(jnp.int32) * CLUSTERS + cluster_ids
        picked = jnp.argsort(order_score, stable=True)[:SAMPLES].astype(jnp.int32)
        shuffle = jax.random.permutation(key_shuffle, SAMPLES)
        return picked[shuffle].astype(jnp.int32)
    block_keys = jax.random.split(key, BLOCKS)
    return jax.vmap(one_block)(block_keys)


def draw_item_bias(key, part):
    key_base = jax.random.fold_in(key, 0)
    values_out = jnp.clip(jax.random.normal(key_base, (ITEMS,), jnp.float32), -4.0, 4.0)
    return values_out.astype(jnp.bfloat16)


def place_ends(values, rng, low, largest):
    longest = values.shape.index(max(values.shape))
    spots = []
    for shift in (0, 1):
        where = [jax.random.randint(jax.random.fold_in(rng, axis), (), 0, length) for axis, length in enumerate(values.shape)]
        where[longest] = (where[longest] + shift) % values.shape[longest]
        spots.append(tuple(where))
    return values.at[spots[0]].set(low).at[spots[1]].set(largest)


def block_levels(own_key, extent, pieces, least, top_value):
    factor_of = 1.0
    for position, blocks in pieces:
        draws = jax.random.uniform(jax.random.fold_in(jax.random.fold_in(own_key, 6), position), (blocks,), jnp.float32, least / len(pieces), top_value / len(pieces))
        factor_of = factor_of * jnp.repeat(jnp.exp(draws), extent[position] // blocks).reshape((-1,) + (1,) * (len(extent) - 1 - position))
    return factor_of


def gaussian(rng, shape, spread, reach, cuts=(), held_as=jnp.bfloat16):
    drawn = spread * jax.random.normal(rng, shape, jnp.float32)
    if cuts:
        drawn = drawn * block_levels(rng, shape, cuts, -0.22, 0.18)
    return jnp.clip(drawn, -reach, reach).astype(held_as)


def setup_inputs(seed: int = 0) -> dict:
    splits = jax.random.split(jax.random.key(seed), 7)
    user_emb = gaussian(splits[0], (USERS, DE), 0.0625, 0.375, ((0, 32),))
    samples = draw_samples(jax.random.fold_in(splits[6], 71), 0)
    pos_item = place_ends(jax.random.randint(splits[2], (USERS,), 0, ITEMS), jax.random.fold_in(splits[2], 1), 0, ITEMS - 1).astype(jnp.int32)
    item_feat = gaussian(splits[3], (ITEMS, F), 0.03125, 0.1875, ((0, 512),))
    tower_w = gaussian(splits[4], (F, DE), 1.0, 5.0)
    item_bias = draw_item_bias(jax.random.fold_in(splits[6], 71), 0)
    return dict(user_emb=user_emb, samples=samples, pos_item=pos_item, item_feat=item_feat, tower_w=tower_w, item_bias=item_bias)


def reference(user_emb, samples, pos_item, item_feat, tower_w, item_bias):
    item_emb = jnp.dot(item_feat, tower_w, preferred_element_type=jnp.float32).astype(jnp.bfloat16)
    emb_tiles = item_emb.reshape(CLUSTERS, CL, DE)
    bias_float = item_bias.astype(jnp.float32)
    bias_tiles = bias_float.reshape(CLUSTERS, CL)
    user_blocks = user_emb.reshape(BLOCKS, BU, DE)
    pos_blocks = pos_item.reshape(BLOCKS, BU)
    offsets = jnp.arange(CL, dtype=jnp.int32)

    def block_step(item_grad, inputs):
        user_rows, cluster_ids, pos_ids = inputs
        user_float = user_rows.astype(jnp.float32)
        picked = emb_tiles[cluster_ids].astype(jnp.float32)
        logit = jnp.einsum("ud,scd->usc", user_float, picked) + bias_tiles[cluster_ids][None]
        pos_rows = item_emb[pos_ids].astype(jnp.float32)
        pos_logit = jnp.sum(user_float * pos_rows, axis=1) + bias_float[pos_ids]
        row_peak = jnp.maximum(jnp.max(logit, axis=(1, 2)), pos_logit)
        exp_total = jnp.sum(jnp.exp(logit - row_peak[:, None, None]), axis=(1, 2)) + jnp.exp(pos_logit - row_peak)
        log_total = row_peak + jnp.log(exp_total)
        user_loss = log_total - pos_logit
        soft_weight = jnp.exp(logit - log_total[:, None, None]).astype(jnp.bfloat16).astype(jnp.float32)
        pos_weight = jnp.exp(pos_logit - log_total) - 1.0
        user_grad = jnp.einsum("usc,scd->ud", soft_weight, picked) + pos_weight[:, None] * pos_rows
        contrib = jnp.einsum("usc,ud->scd", soft_weight, user_float)
        row_ids = (cluster_ids[:, None] * CL + offsets[None, :]).reshape(-1)
        item_grad = item_grad.at[row_ids].add(contrib.reshape(-1, DE))
        item_grad = item_grad.at[pos_ids].add(pos_weight[:, None] * user_float)
        return item_grad, (user_loss, user_grad)

    item_grad, (user_loss, user_grad) = lax.scan(block_step, jnp.zeros((ITEMS, DE), jnp.float32), (user_blocks, samples, pos_blocks))
    weight_grad = jnp.dot(item_feat.astype(jnp.float32).T, item_grad, precision=lax.Precision.HIGHEST)
    return user_loss.reshape(USERS), user_grad.reshape(USERS, DE), weight_grad
```

```python
import jax
import jax.numpy as jnp
from jax import lax
from jax.experimental import pallas as pl
from jax.experimental.pallas import tpu as pltpu
from jax.sharding import PartitionSpec as P

CL = 128
BU = 128
STEP = 256
NEG = -1e30
FLOOR = -1e29
NT = (((1,), (1,)), ((), ()))
f32 = jnp.float32
bf16 = jnp.bfloat16


def spread(x, axis, n):
    return lax.all_to_all(jnp.broadcast_to(x[None], (n,) + x.shape), axis, 0, 0)


def logits_of(item_ref, user_ref, mask_ref):
    width = user_ref.shape[1]
    raw = lax.dot_general(item_ref[:, :width], user_ref[...], NT, preferred_element_type=f32)
    bias = item_ref[:, width:].astype(f32)
    raw = raw + jnp.concatenate([bias] * (STEP // CL), axis=1)
    parts = [raw[c * CL : (c + 1) * CL] + mask_ref[c : c + 1, :] for c in range(raw.shape[0] // CL)]
    return raw, jnp.concatenate(parts, axis=0)


def at_positive(raw, pos_ref):
    return lax.broadcasted_iota(jnp.int32, raw.shape, 0) == pos_ref[...]


def forward(item_ref, user_ref, mask_ref, pos_ref, stat_ref):
    step = pl.program_id(0)
    raw, kept = logits_of(item_ref, user_ref, mask_ref)
    here = (pos_ref[...] >= 0) & (pos_ref[...] < raw.shape[0])
    pos = jnp.sum(jnp.where(at_positive(raw, pos_ref), raw, 0.0), axis=0, keepdims=True)
    pos = jnp.where(here, pos, NEG)
    peak = jnp.maximum(jnp.maximum(jnp.max(kept, axis=0, keepdims=True), pos), FLOOR)
    total = jnp.sum(jnp.exp(kept - peak), axis=0, keepdims=True) + jnp.exp(pos - peak)
    lse = jnp.where(total > 0.0, peak + jnp.log(jnp.maximum(total, 1e-37)), NEG)
    blocks = stat_ref.shape[0] // 2
    for h in range(STEP // BU):
        row = step * (STEP // BU) + h
        stat_ref[pl.ds(row, 1), :] = lse[:, h * BU : (h + 1) * BU]
        stat_ref[pl.ds(blocks + row, 1), :] = pos[:, h * BU : (h + 1) * BU]


def backward(item_ref, user_ref, mask_ref, pos_ref, stat_ref, grad_ref, high_ref, loss_ref, item_t, total_ref, weight_ref, sums):
    step = pl.program_id(0)
    width = user_ref.shape[1]
    blocks = loss_ref.shape[0]

    @pl.when(step == 0)
    def _():
        lse = stat_ref[:, :blocks, :]
        peak = jnp.max(lse, axis=0)
        total = peak + jnp.log(jnp.sum(jnp.exp(lse - peak[None]), axis=0))
        pos = jnp.max(stat_ref[:, blocks:, :], axis=0)
        total_ref[...] = total
        loss_ref[...] = total - pos
        weight_ref[...] = jnp.exp(pos - total) - 1.0
        item_t[...] = item_ref[:, :width].astype(f32).T.astype(bf16)
        sums[...] = jnp.zeros_like(sums)

    def row_of(ref):
        rows = [ref[pl.ds(step * (STEP // BU) + h, 1), :] for h in range(STEP // BU)]
        return jnp.concatenate(rows, axis=1)

    raw, kept = logits_of(item_ref, user_ref, mask_ref)
    soft = jnp.exp(kept - row_of(total_ref))
    soft = soft + jnp.where(at_positive(raw, pos_ref), row_of(weight_ref), 0.0)
    soft = soft.astype(bf16)
    sums[...] += jnp.dot(soft, user_ref[...], preferred_element_type=f32)
    grad_ref[...] = jnp.dot(item_t[...], soft, preferred_element_type=f32).T.astype(bf16)

    @pl.when(step == pl.num_programs(0) - 1)
    def _():
        high = sums[...].astype(bf16)
        high_ref[:, :width] = high
        high_ref[:, width:] = (sums[...] - high.astype(f32)).astype(bf16)


def body(user_emb, samples, pos_item, item_feat, tower_w, item_bias):
    group, shards = lax.axis_size("users"), lax.axis_size("items")
    shard = lax.axis_index("items")
    own, width = item_feat.shape[0], tower_w.shape[1]
    rows = own * group
    clus = rows // CL
    users, blocks = user_emb.shape[0], samples.shape[0]
    steps = users // STEP

    own_emb = jnp.dot(item_feat, tower_w, preferred_element_type=f32).astype(bf16)
    packed = jnp.concatenate([own_emb, jnp.broadcast_to(item_bias[:, None], (own, CL))], axis=1)
    items = spread(packed, "users", group).reshape(rows, width + CL)
    feats = lax.all_gather(item_feat, "users", axis=0, tiled=True)

    ids = shard * clus + jnp.arange(clus, dtype=jnp.int32)
    taken = jnp.any(samples[None] == ids[:, None, None], axis=2)
    mask = jnp.repeat(jnp.where(taken, 0.0, NEG).astype(f32), BU, axis=1)
    pos_row = (pos_item - shard * rows).reshape(1, users)

    in_specs = [
        pl.BlockSpec((rows, width + CL), lambda i: (0, 0)),
        pl.BlockSpec((STEP, width), lambda i: (i, 0)),
        pl.BlockSpec((clus, STEP), lambda i: (0, i)),
        pl.BlockSpec((1, STEP), lambda i: (0, i)),
    ]
    params = pltpu.CompilerParams(vmem_limit_bytes=40 << 20)
    stat = pl.pallas_call(
        forward,
        grid=(steps,),
        in_specs=in_specs,
        out_specs=pl.BlockSpec((2 * blocks, BU), lambda i: (0, 0)),
        out_shape=jax.ShapeDtypeStruct((2 * blocks, BU), f32),
        compiler_params=params,
    )(items, user_emb, mask, pos_row)
    stats = spread(stat, "items", shards)
    grad, high, loss = pl.pallas_call(
        backward,
        grid=(steps,),
        in_specs=in_specs + [pl.BlockSpec((shards, 2 * blocks, BU), lambda i: (0, 0, 0))],
        out_specs=[
            pl.BlockSpec((STEP, width), lambda i: (i, 0)),
            pl.BlockSpec((rows, 2 * width), lambda i: (0, 0)),
            pl.BlockSpec((blocks, BU), lambda i: (0, 0)),
        ],
        out_shape=[
            jax.ShapeDtypeStruct((users, width), bf16),
            jax.ShapeDtypeStruct((rows, 2 * width), bf16),
            jax.ShapeDtypeStruct((blocks, BU), f32),
        ],
        scratch_shapes=[
            pltpu.VMEM((width, rows), bf16),
            pltpu.VMEM((blocks, BU), f32),
            pltpu.VMEM((blocks, BU), f32),
            pltpu.VMEM((rows, width), f32),
        ],
        compiler_params=params,
    )(items, user_emb, mask, pos_row, stats)

    part = lax.dot_general(feats, high, (((0,), (0,)), ((), ())), preferred_element_type=f32)
    part = (part[:, :width] + part[:, width:]).astype(bf16)
    cut = part.shape[0] // group
    part = lax.all_to_all(part.reshape(group, cut, width), "users", 0, 0)
    part = jnp.sum(part.astype(f32), axis=0).astype(bf16)
    part = jnp.sum(spread(part, "items", shards).astype(f32), axis=0).astype(bf16)
    weight_grad = spread(part, "users", group).reshape(group * cut, width).astype(f32)

    grad = lax.all_to_all(grad.reshape(shards, users // shards, width), "items", 0, 0)
    user_grad = jnp.sum(grad.astype(f32), axis=0)
    return loss.reshape(users), user_grad, weight_grad


def solution(mesh):
    return jax.shard_map(
        body,
        mesh=mesh,
        in_specs=(
            P("users", None),
            P("users", None),
            P("users"),
            P(("items", "users"), None),
            P(),
            P(("items", "users")),
        ),
        out_specs=(P("users"), P(("users", "items"), None), P()),
        check_vma=False,
    )
```

```python
import jax
import jax.numpy as jnp
from jax import lax
from jax.experimental import pallas as pl
from jax.experimental.pallas import tpu as pltpu
from jax.sharding import PartitionSpec as P

CL = 128
BU = 128
STEP = 256
NEG = -1e30
FLOOR = -1e29
NT = (((1,), (1,)), ((), ()))
f32 = jnp.float32
bf16 = jnp.bfloat16


def spread(x, axis, n):
    return lax.all_to_all(jnp.broadcast_to(x[None], (n,) + x.shape), axis, 0, 0)


def logits_of(item_ref, user_ref, mask_ref):
    width = user_ref.shape[1]
    raw = lax.dot_general(item_ref[:, :width], user_ref[...], NT, preferred_element_type=f32)
    bias = item_ref[:, width:].astype(f32)
    raw = raw + jnp.concatenate([bias] * (STEP // CL), axis=1)
    parts = [raw[c * CL : (c + 1) * CL] + mask_ref[c : c + 1, :] for c in range(raw.shape[0] // CL)]
    return raw, jnp.concatenate(parts, axis=0)


def at_positive(raw, pos_ref):
    return lax.broadcasted_iota(jnp.int32, raw.shape, 0) == pos_ref[...]


def forward(item_ref, user_ref, mask_ref, pos_ref, stat_ref):
    step = pl.program_id(0)
    raw, kept = logits_of(item_ref, user_ref, mask_ref)
    here = (pos_ref[...] >= 0) & (pos_ref[...] < raw.shape[0])
    pos = jnp.sum(jnp.where(at_positive(raw, pos_ref), raw, 0.0), axis=0, keepdims=True)
    pos = jnp.where(here, pos, NEG)
    peak = jnp.maximum(jnp.maximum(jnp.max(kept, axis=0, keepdims=True), pos), FLOOR)
    total = jnp.sum(jnp.exp(kept - peak), axis=0, keepdims=True) + jnp.exp(pos - peak)
    lse = jnp.where(total > 0.0, peak + jnp.log(jnp.maximum(total, 1e-37)), NEG)
    blocks = stat_ref.shape[0] // 2
    for h in range(STEP // BU):
        row = step * (STEP // BU) + h
        stat_ref[pl.ds(row, 1), :] = lse[:, h * BU : (h + 1) * BU]
        stat_ref[pl.ds(blocks + row, 1), :] = pos[:, h * BU : (h + 1) * BU]


def backward(shard_ref, item_ref, user_ref, mask_ref, pos_ref, stat_ref, *refs):
    *grad_refs, high_ref, loss_ref, item_t, total_ref, weight_ref, sums = refs
    step = pl.program_id(0)
    width = user_ref.shape[1]
    blocks = loss_ref.shape[0]

    @pl.when(step == 0)
    def _():
        lse = stat_ref[:, :blocks, :]
        peak = jnp.max(lse, axis=0)
        total = peak + jnp.log(jnp.sum(jnp.exp(lse - peak[None]), axis=0))
        pos = jnp.max(stat_ref[:, blocks:, :], axis=0)
        total_ref[...] = total
        loss_ref[...] = total - pos
        weight_ref[...] = jnp.exp(pos - total) - 1.0
        item_t[...] = item_ref[:, :width].astype(f32).T.astype(bf16)
        sums[...] = jnp.zeros_like(sums)

    def row_of(ref):
        rows = [ref[pl.ds(step * (STEP // BU) + h, 1), :] for h in range(STEP // BU)]
        return jnp.concatenate(rows, axis=1)

    raw, kept = logits_of(item_ref, user_ref, mask_ref)
    soft = jnp.exp(kept - row_of(total_ref))
    soft = soft + jnp.where(at_positive(raw, pos_ref), row_of(weight_ref), 0.0)
    soft = soft.astype(bf16)
    sums[...] += jnp.dot(soft, user_ref[...], preferred_element_type=f32)
    grad = jnp.dot(item_t[...], soft, preferred_element_type=f32).T.astype(bf16)
    span = len(grad_refs)
    for h in range(STEP // BU):
        away = lax.rem(step * (STEP // BU) + h - shard_ref[0] + span, span)
        for shift, grad_ref in enumerate(grad_refs):

            @pl.when(away == shift)
            def _():
                grad_ref[...] = grad[h * BU : (h + 1) * BU]

    @pl.when(step == pl.num_programs(0) - 1)
    def _():
        high = sums[...].astype(bf16)
        high_ref[:, :width] = high
        high_ref[:, width:] = (sums[...] - high.astype(f32)).astype(bf16)


def body(user_emb, samples, pos_item, item_feat, tower_w, item_bias):
    group, shards = lax.axis_size("users"), lax.axis_size("items")
    shard = lax.axis_index("items")
    own, width = item_feat.shape[0], tower_w.shape[1]
    rows = own * group
    clus = rows // CL
    users, blocks = user_emb.shape[0], samples.shape[0]
    steps = users // STEP

    own_emb = jnp.dot(item_feat, tower_w, preferred_element_type=f32).astype(bf16)
    packed = jnp.concatenate([own_emb, jnp.broadcast_to(item_bias[:, None], (own, CL))], axis=1)
    items = spread(packed, "users", group).reshape(rows, width + CL)
    feats = lax.all_gather(item_feat, "users", axis=0, tiled=True)

    ids = shard * clus + jnp.arange(clus, dtype=jnp.int32)
    taken = jnp.any(samples[None] == ids[:, None, None], axis=2)
    mask = jnp.repeat(jnp.where(taken, 0.0, NEG).astype(f32), BU, axis=1)
    pos_row = (pos_item - shard * rows).reshape(1, users)

    in_specs = [
        pl.BlockSpec((rows, width + CL), lambda i: (0, 0)),
        pl.BlockSpec((STEP, width), lambda i: (i, 0)),
        pl.BlockSpec((clus, STEP), lambda i: (0, i)),
        pl.BlockSpec((1, STEP), lambda i: (0, i)),
    ]
    params = pltpu.CompilerParams(vmem_limit_bytes=40 << 20)
    stat = pl.pallas_call(
        forward,
        grid=(steps,),
        in_specs=in_specs,
        out_specs=pl.BlockSpec((2 * blocks, BU), lambda i: (0, 0)),
        out_shape=jax.ShapeDtypeStruct((2 * blocks, BU), f32),
        compiler_params=params,
    )(items, user_emb, mask, pos_row)
    stats = spread(stat, "items", shards)
    *grads, high, loss = pl.pallas_call(
        backward,
        grid=(steps,),
        in_specs=[pl.BlockSpec(memory_space=pltpu.SMEM)]
        + in_specs
        + [pl.BlockSpec((shards, 2 * blocks, BU), lambda i: (0, 0, 0))],
        out_specs=[pl.BlockSpec((BU, width), lambda i: (0, 0))] * shards
        + [
            pl.BlockSpec((rows, 2 * width), lambda i: (0, 0)),
            pl.BlockSpec((blocks, BU), lambda i: (0, 0)),
        ],
        out_shape=[jax.ShapeDtypeStruct((BU, width), bf16)] * shards
        + [
            jax.ShapeDtypeStruct((rows, 2 * width), bf16),
            jax.ShapeDtypeStruct((blocks, BU), f32),
        ],
        scratch_shapes=[
            pltpu.VMEM((width, rows), bf16),
            pltpu.VMEM((blocks, BU), f32),
            pltpu.VMEM((blocks, BU), f32),
            pltpu.VMEM((rows, width), f32),
        ],
        compiler_params=params,
    )(jnp.reshape(shard, (1,)), items, user_emb, mask, pos_row, stats)
    for shift in range(1, shards):
        pairs = [(k, (k + shift) % shards) for k in range(shards)]
        grads[shift] = lax.ppermute(grads[shift], "items", pairs)

    part = lax.dot_general(feats, high, (((0,), (0,)), ((), ())), preferred_element_type=f32)
    part = (part[:, :width] + part[:, width:]).astype(bf16)
    cut = part.shape[0] // group
    part = lax.all_to_all(part.reshape(group, cut, width), "users", 0, 0)
    part = jnp.sum(part.astype(f32), axis=0).astype(bf16)
    part = jnp.sum(spread(part, "items", shards).astype(f32), axis=0).astype(bf16)
    weight_grad = spread(part, "users", group).reshape(group * cut, width).astype(f32)

    user_grad = sum(grad.astype(f32) for grad in grads)
    return loss.reshape(users), user_grad, weight_grad


def solution(mesh):
    return jax.shard_map(
        body,
        mesh=mesh,
        in_specs=(
            P("users", None),
            P("users", None),
            P("users"),
            P(("items", "users"), None),
            P(),
            P(("items", "users")),
        ),
        out_specs=(P("users"), P(("users", "items"), None), P()),
        check_vma=False,
    )
```

```python
import jax
import jax.numpy as jnp
from jax import lax
from jax.experimental import pallas as pl
from jax.experimental.pallas import tpu as pltpu
from jax.sharding import PartitionSpec as P

CL = 128
BU = 128
STEP = 256
NEG = -1e30
FLOOR = -1e29
NT = (((1,), (1,)), ((), ()))
f32 = jnp.float32
bf16 = jnp.bfloat16


def spread(x, axis, n):
    return lax.all_to_all(jnp.broadcast_to(x[None], (n,) + x.shape), axis, 0, 0)


def logits_of(item_ref, user_ref, mask_ref):
    width = user_ref.shape[1]
    raw = lax.dot_general(item_ref[:, :width], user_ref[...], NT, preferred_element_type=f32)
    bias = item_ref[:, width:].astype(f32)
    raw = raw + jnp.concatenate([bias] * (STEP // CL), axis=1)
    parts = [raw[c * CL : (c + 1) * CL] + mask_ref[c : c + 1, :] for c in range(raw.shape[0] // CL)]
    return raw, jnp.concatenate(parts, axis=0)


def at_positive(raw, pos_ref):
    return lax.broadcasted_iota(jnp.int32, raw.shape, 0) == pos_ref[...]


def forward(item_ref, user_ref, mask_ref, pos_ref, stat_ref):
    step = pl.program_id(0)
    raw, kept = logits_of(item_ref, user_ref, mask_ref)
    here = (pos_ref[...] >= 0) & (pos_ref[...] < raw.shape[0])
    pos = jnp.sum(jnp.where(at_positive(raw, pos_ref), raw, 0.0), axis=0, keepdims=True)
    pos = jnp.where(here, pos, NEG)
    peak = jnp.maximum(jnp.maximum(jnp.max(kept, axis=0, keepdims=True), pos), FLOOR)
    total = jnp.sum(jnp.exp(kept - peak), axis=0, keepdims=True) + jnp.exp(pos - peak)
    lse = jnp.where(total > 0.0, peak + jnp.log(jnp.maximum(total, 1e-37)), NEG)
    blocks = stat_ref.shape[0] // 2
    for h in range(STEP // BU):
        row = step * (STEP // BU) + h
        stat_ref[pl.ds(row, 1), :] = lse[:, h * BU : (h + 1) * BU]
        stat_ref[pl.ds(blocks + row, 1), :] = pos[:, h * BU : (h + 1) * BU]


def backward(item_ref, user_ref, mask_ref, pos_ref, stat_ref, grad_ref, high_ref, loss_ref, item_t, total_ref, weight_ref, sums):
    step = pl.program_id(0)
    width = user_ref.shape[1]
    blocks = loss_ref.shape[0]

    @pl.when(step == 0)
    def _():
        lse = stat_ref[:, :blocks, :]
        peak = jnp.max(lse, axis=0)
        total = peak + jnp.log(jnp.sum(jnp.exp(lse - peak[None]), axis=0))
        pos = jnp.max(stat_ref[:, blocks:, :], axis=0)
        total_ref[...] = total
        loss_ref[...] = total - pos
        weight_ref[...] = jnp.exp(pos - total) - 1.0
        item_t[...] = item_ref[:, :width].astype(f32).T.astype(bf16)
        sums[...] = jnp.zeros_like(sums)

    def row_of(ref):
        rows = [ref[pl.ds(step * (STEP // BU) + h, 1), :] for h in range(STEP // BU)]
        return jnp.concatenate(rows, axis=1)

    raw, kept = logits_of(item_ref, user_ref, mask_ref)
    soft = jnp.exp(kept - row_of(total_ref))
    soft = soft + jnp.where(at_positive(raw, pos_ref), row_of(weight_ref), 0.0)
    soft = soft.astype(bf16)
    sums[...] += jnp.dot(soft, user_ref[...], preferred_element_type=f32)
    grad_ref[...] = jnp.dot(item_t[...], soft, preferred_element_type=f32).T

    @pl.when(step == pl.num_programs(0) - 1)
    def _():
        high = sums[...].astype(bf16)
        high_ref[:, :width] = high
        high_ref[:, width:] = (sums[...] - high.astype(f32)).astype(bf16)


def body(user_emb, samples, pos_item, item_feat, tower_w, item_bias):
    group, shards = lax.axis_size("users"), lax.axis_size("items")
    shard = lax.axis_index("items")
    own, width = item_feat.shape[0], tower_w.shape[1]
    rows = own * group
    clus = rows // CL
    users, blocks = user_emb.shape[0], samples.shape[0]
    steps = users // STEP

    own_emb = jnp.dot(item_feat, tower_w, preferred_element_type=f32).astype(bf16)
    packed = jnp.concatenate([own_emb, jnp.broadcast_to(item_bias[:, None], (own, CL))], axis=1)
    items = spread(packed, "users", group).reshape(rows, width + CL)
    feats = lax.all_gather(item_feat, "users", axis=0, tiled=True)

    ids = shard * clus + jnp.arange(clus, dtype=jnp.int32)
    taken = jnp.any(samples[None] == ids[:, None, None], axis=2)
    mask = jnp.repeat(jnp.where(taken, 0.0, NEG).astype(f32), BU, axis=1)
    pos_row = (pos_item - shard * rows).reshape(1, users)

    in_specs = [
        pl.BlockSpec((rows, width + CL), lambda i: (0, 0)),
        pl.BlockSpec((STEP, width), lambda i: (i, 0)),
        pl.BlockSpec((clus, STEP), lambda i: (0, i)),
        pl.BlockSpec((1, STEP), lambda i: (0, i)),
    ]
    params = pltpu.CompilerParams(vmem_limit_bytes=40 << 20)
    stat = pl.pallas_call(
        forward,
        grid=(steps,),
        in_specs=in_specs,
        out_specs=pl.BlockSpec((2 * blocks, BU), lambda i: (0, 0)),
        out_shape=jax.ShapeDtypeStruct((2 * blocks, BU), f32),
        compiler_params=params,
    )(items, user_emb, mask, pos_row)
    stats = spread(stat, "items", shards)
    grad, high, loss = pl.pallas_call(
        backward,
        grid=(steps,),
        in_specs=in_specs + [pl.BlockSpec((shards, 2 * blocks, BU), lambda i: (0, 0, 0))],
        out_specs=[
            pl.BlockSpec((STEP, width), lambda i: (i, 0)),
            pl.BlockSpec((rows, 2 * width), lambda i: (0, 0)),
            pl.BlockSpec((blocks, BU), lambda i: (0, 0)),
        ],
        out_shape=[
            jax.ShapeDtypeStruct((users, width), f32),
            jax.ShapeDtypeStruct((rows, 2 * width), bf16),
            jax.ShapeDtypeStruct((blocks, BU), f32),
        ],
        scratch_shapes=[
            pltpu.VMEM((width, rows), bf16),
            pltpu.VMEM((blocks, BU), f32),
            pltpu.VMEM((blocks, BU), f32),
            pltpu.VMEM((rows, width), f32),
        ],
        compiler_params=params,
    )(items, user_emb, mask, pos_row, stats)

    user_grad = lax.psum_scatter(grad, "items", scatter_dimension=0, tiled=True)

    part = lax.dot_general(feats, high, (((0,), (0,)), ((), ())), preferred_element_type=f32)
    part = (part[:, :width] + part[:, width:]).astype(bf16)
    cut = part.shape[0] // group
    part = lax.all_to_all(part.reshape(group, cut, width), "users", 0, 0)
    part = jnp.sum(part.astype(f32), axis=0).astype(bf16)
    part = jnp.sum(spread(part, "items", shards).astype(f32), axis=0).astype(bf16)
    weight_grad = spread(part, "users", group).reshape(group * cut, width).astype(f32)

    return loss.reshape(users), user_grad, weight_grad


def solution(mesh):
    return jax.shard_map(
        body,
        mesh=mesh,
        in_specs=(
            P("users", None),
            P("users", None),
            P("users"),
            P(("items", "users"), None),
            P(),
            P(("items", "users")),
        ),
        out_specs=(P("users"), P(("users", "items"), None), P()),
        check_vma=False,
    )
```

```python
import jax
import jax.numpy as jnp
from jax import lax
from jax.experimental import pallas as pl
from jax.experimental.pallas import tpu as pltpu
from jax.sharding import PartitionSpec as P

CL = 128
BU = 128
STEP = 1024
NEG = -1e30
FLOOR = -1e29
PIECES = 3
NT = (((1,), (1,)), ((), ()))
f32 = jnp.float32
bf16 = jnp.bfloat16


def spread(x, axis, n):
    return lax.all_to_all(jnp.broadcast_to(x[None], (n,) + x.shape), axis, 0, 0)


def logits_of(item_ref, user_ref, mask_ref):
    width = user_ref.shape[1]
    raw = lax.dot_general(item_ref[:, :width], user_ref[...], NT, preferred_element_type=f32)
    bias = item_ref[:, width:].astype(f32)
    raw = raw + jnp.concatenate([bias] * (STEP // CL), axis=1)
    parts = [raw[c * CL : (c + 1) * CL] + mask_ref[c : c + 1, :] for c in range(raw.shape[0] // CL)]
    return raw, jnp.concatenate(parts, axis=0)


def at_positive(raw, pos_ref):
    return lax.broadcasted_iota(jnp.int32, raw.shape, 0) == pos_ref[...]


def forward(item_ref, user_ref, mask_ref, pos_ref, lse_ref, own_ref, split_ref):
    step = pl.program_id(0)
    raw, kept = logits_of(item_ref, user_ref, mask_ref)
    here = (pos_ref[...] >= 0) & (pos_ref[...] < raw.shape[0])
    pos = jnp.sum(jnp.where(at_positive(raw, pos_ref), raw, 0.0), axis=0, keepdims=True)
    pos = jnp.where(here, pos, NEG)
    peak = jnp.maximum(jnp.maximum(jnp.max(kept, axis=0, keepdims=True), pos), FLOOR)
    total = jnp.sum(jnp.exp(kept - peak), axis=0, keepdims=True) + jnp.exp(pos - peak)
    lse = jnp.where(total > 0.0, peak + jnp.log(jnp.maximum(total, 1e-37)), NEG)
    for h in range(STEP // BU):
        row = step * (STEP // BU) + h
        lse_ref[pl.ds(row, 1), :] = lse[:, h * BU : (h + 1) * BU]
        own_ref[pl.ds(row, 1), :] = pos[:, h * BU : (h + 1) * BU]
    rest = jnp.where(here, pos, 0.0)
    width = split_ref.shape[1]
    for k in range(PIECES):
        piece = rest.astype(bf16).astype(f32)
        rest = rest - piece
        for h in range(STEP // width):
            row = k * (split_ref.shape[0] // PIECES) + step * (STEP // width) + h
            split_ref[pl.ds(row, 1), :] = piece[:, h * width : (h + 1) * width]


def backward(item_ref, user_ref, mask_ref, pos_ref, lses_ref, own_ref, grad_ref, high_ref, total_ref, item_t, weight_ref, sums):
    step = pl.program_id(0)
    width = user_ref.shape[1]

    @pl.when(step == 0)
    def _():
        lse = lses_ref[...]
        peak = jnp.max(lse, axis=0)
        total = peak + jnp.log(jnp.sum(jnp.exp(lse - peak[None]), axis=0))
        total_ref[...] = total
        weight_ref[...] = jnp.exp(own_ref[...] - total) - 1.0
        item_t[...] = item_ref[:, :width].astype(f32).T.astype(bf16)
        sums[...] = jnp.zeros_like(sums)

    def row_of(ref):
        rows = [ref[pl.ds(step * (STEP // BU) + h, 1), :] for h in range(STEP // BU)]
        return jnp.concatenate(rows, axis=1)

    raw, kept = logits_of(item_ref, user_ref, mask_ref)
    soft = jnp.exp(kept - row_of(total_ref))
    soft = soft + jnp.where(at_positive(raw, pos_ref), row_of(weight_ref), 0.0)
    soft = soft.astype(bf16)
    sums[...] += jnp.dot(soft, user_ref[...], preferred_element_type=f32)
    grad_ref[...] = jnp.dot(item_t[...], soft, preferred_element_type=f32).T

    @pl.when(step == pl.num_programs(0) - 1)
    def _():
        high = sums[...].astype(bf16)
        high_ref[:, :width] = high
        high_ref[:, width:] = (sums[...] - high.astype(f32)).astype(bf16)


def body(user_emb, samples, pos_item, item_feat, tower_w, item_bias):
    group, shards = lax.axis_size("users"), lax.axis_size("items")
    shard = lax.axis_index("items")
    own, width = item_feat.shape[0], tower_w.shape[1]
    rows = own * group
    clus = rows // CL
    users, blocks = user_emb.shape[0], samples.shape[0]
    steps = users // STEP

    own_emb = jnp.dot(item_feat, tower_w, preferred_element_type=f32).astype(bf16)
    packed = jnp.concatenate([own_emb, jnp.broadcast_to(item_bias[:, None], (own, CL))], axis=1)
    items = spread(packed, "users", group).reshape(rows, width + CL)
    feats = lax.all_gather(item_feat, "users", axis=0, tiled=True)

    ids = shard * clus + jnp.arange(clus, dtype=jnp.int32)
    taken = jnp.any(samples[None] == ids[:, None, None], axis=2)
    mask = jnp.repeat(jnp.where(taken, 0.0, NEG).astype(f32), BU, axis=1)
    pos_row = (pos_item - shard * rows).reshape(1, users)

    in_specs = [
        pl.BlockSpec((rows, width + CL), lambda i: (0, 0)),
        pl.BlockSpec((STEP, width), lambda i: (i, 0)),
        pl.BlockSpec((clus, STEP), lambda i: (0, i)),
        pl.BlockSpec((1, STEP), lambda i: (0, i)),
    ]
    params = pltpu.CompilerParams(vmem_limit_bytes=48 << 20)
    table = pl.BlockSpec((blocks, BU), lambda i: (0, 0))
    pieces = PIECES * users // width
    lse, own_pos, split = pl.pallas_call(
        forward,
        grid=(steps,),
        in_specs=in_specs,
        out_specs=[table, table, pl.BlockSpec((pieces, width), lambda i: (0, 0))],
        out_shape=[
            jax.ShapeDtypeStruct((blocks, BU), f32),
            jax.ShapeDtypeStruct((blocks, BU), f32),
            jax.ShapeDtypeStruct((pieces, width), f32),
        ],
        compiler_params=params,
    )(items, user_emb, mask, pos_row)
    lses = spread(lse, "items", shards)
    grad, high, total = pl.pallas_call(
        backward,
        grid=(steps,),
        in_specs=in_specs + [pl.BlockSpec((shards, blocks, BU), lambda i: (0, 0, 0)), table],
        out_specs=[
            pl.BlockSpec((STEP, width), lambda i: (i, 0)),
            pl.BlockSpec((rows, 2 * width), lambda i: (0, 0)),
            table,
        ],
        out_shape=[
            pltpu.HBM((users, width), f32),
            jax.ShapeDtypeStruct((rows, 2 * width), bf16),
            jax.ShapeDtypeStruct((blocks, BU), f32),
        ],
        scratch_shapes=[
            pltpu.VMEM((width, rows), bf16),
            pltpu.VMEM((blocks, BU), f32),
            pltpu.VMEM((rows, width), f32),
        ],
        compiler_params=params,
    )(items, user_emb, mask, pos_row, lses, own_pos)

    user_grad = lax.psum_scatter(grad, "items", scatter_dimension=0, tiled=True)

    part = lax.dot_general(feats, high, (((0,), (0,)), ((), ())), preferred_element_type=f32)
    part = (part[:, :width] + part[:, width:]).astype(bf16)
    cut = part.shape[0] // group
    part = lax.all_to_all(part.reshape(group, cut, width), "users", 0, 0)
    part = jnp.sum(part.astype(f32), axis=0).astype(bf16)
    both = spread(jnp.concatenate([part, split.astype(bf16)], axis=0), "items", shards)
    both = jnp.sum(both.astype(f32), axis=0)
    weight_grad = spread(both[:cut].astype(bf16), "users", group).reshape(group * cut, width).astype(f32)
    pos_logit = jnp.sum(both[cut:].reshape(PIECES, users), axis=0)
    user_loss = total.reshape(users) - pos_logit
    return user_loss, user_grad, weight_grad


def solution(mesh):
    return jax.shard_map(
        body,
        mesh=mesh,
        in_specs=(
            P("users", None),
            P("users", None),
            P("users"),
            P(("items", "users"), None),
            P(),
            P(("items", "users")),
        ),
        out_specs=(P("users"), P(("users", "items"), None), P()),
        check_vma=False,
    )
```

```python
import jax
import jax.numpy as jnp
from jax import lax
from jax.experimental import pallas as pl
from jax.experimental.pallas import tpu as pltpu
from jax.sharding import PartitionSpec as P

CL = 128
BU = 128
STEP = 1024
NEG = -1e30
FLOOR = -1e29
NT = (((1,), (1,)), ((), ()))
f32 = jnp.float32
bf16 = jnp.bfloat16


def spread(x, axis, n):
    return lax.all_to_all(jnp.broadcast_to(x[None], (n,) + x.shape), axis, 0, 0)


def logits_of(item_ref, user_ref, mask_ref):
    width = user_ref.shape[1]
    raw = lax.dot_general(item_ref[:, :width], user_ref[...], NT, preferred_element_type=f32)
    bias = item_ref[:, width:].astype(f32)
    raw = raw + jnp.concatenate([bias] * (STEP // CL), axis=1)
    parts = [raw[c * CL : (c + 1) * CL] + mask_ref[c : c + 1, :] for c in range(raw.shape[0] // CL)]
    return raw, jnp.concatenate(parts, axis=0)


def at_positive(raw, pos_ref):
    return lax.broadcasted_iota(jnp.int32, raw.shape, 0) == pos_ref[...]


def forward(item_ref, user_ref, mask_ref, pos_ref, lse_ref, own_ref, below_ref):
    step = pl.program_id(0)
    raw, kept = logits_of(item_ref, user_ref, mask_ref)
    here = (pos_ref[...] >= 0) & (pos_ref[...] < raw.shape[0])
    pos = jnp.sum(jnp.where(at_positive(raw, pos_ref), raw, 0.0), axis=0, keepdims=True)
    pos = jnp.where(here, pos, NEG)
    peak = jnp.maximum(jnp.maximum(jnp.max(kept, axis=0, keepdims=True), pos), FLOOR)
    total = jnp.sum(jnp.exp(kept - peak), axis=0, keepdims=True) + jnp.exp(pos - peak)
    lse = jnp.where(total > 0.0, peak + jnp.log(jnp.maximum(total, 1e-37)), NEG)
    for h in range(STEP // BU):
        row = step * (STEP // BU) + h
        lse_ref[pl.ds(row, 1), :] = lse[:, h * BU : (h + 1) * BU]
        own_ref[pl.ds(row, 1), :] = pos[:, h * BU : (h + 1) * BU]
    below = jnp.where(here, lse - pos, 0.0)
    width = below_ref.shape[1]
    for h in range(STEP // width):
        below_ref[pl.ds(step * (STEP // width) + h, 1), :] = below[:, h * width : (h + 1) * width]


def backward(item_ref, user_ref, mask_ref, pos_ref, lses_ref, own_ref, owner_ref, grad_ref, high_ref, gap_ref, item_t, total_ref, weight_ref, sums):
    step = pl.program_id(0)
    width = user_ref.shape[1]

    @pl.when(step == 0)
    def _():
        lse = lses_ref[...]
        peak = jnp.max(lse, axis=0)
        total = peak + jnp.log(jnp.sum(jnp.exp(lse - peak[None]), axis=0))
        total_ref[...] = total
        at_owner = lax.broadcasted_iota(jnp.int32, lse.shape, 0) == owner_ref[...][None]
        gap_ref[...] = total - jnp.sum(jnp.where(at_owner, lse, 0.0), axis=0)
        weight_ref[...] = jnp.exp(own_ref[...] - total) - 1.0
        item_t[...] = item_ref[:, :width].astype(f32).T.astype(bf16)
        sums[...] = jnp.zeros_like(sums)

    def row_of(ref):
        rows = [ref[pl.ds(step * (STEP // BU) + h, 1), :] for h in range(STEP // BU)]
        return jnp.concatenate(rows, axis=1)

    raw, kept = logits_of(item_ref, user_ref, mask_ref)
    soft = jnp.exp(kept - row_of(total_ref))
    soft = soft + jnp.where(at_positive(raw, pos_ref), row_of(weight_ref), 0.0)
    soft = soft.astype(bf16)
    sums[...] += jnp.dot(soft, user_ref[...], preferred_element_type=f32)
    grad_ref[...] = jnp.dot(item_t[...], soft, preferred_element_type=f32).T

    @pl.when(step == pl.num_programs(0) - 1)
    def _():
        high = sums[...].astype(bf16)
        high_ref[:, :width] = high
        high_ref[:, width:] = (sums[...] - high.astype(f32)).astype(bf16)


def body(user_emb, samples, pos_item, item_feat, tower_w, item_bias):
    group, shards = lax.axis_size("users"), lax.axis_size("items")
    shard = lax.axis_index("items")
    own, width = item_feat.shape[0], tower_w.shape[1]
    rows = own * group
    clus = rows // CL
    users, blocks = user_emb.shape[0], samples.shape[0]
    steps = users // STEP

    own_emb = jnp.dot(item_feat, tower_w, preferred_element_type=f32).astype(bf16)
    packed = jnp.concatenate([own_emb, jnp.broadcast_to(item_bias[:, None], (own, CL))], axis=1)
    items = spread(packed, "users", group).reshape(rows, width + CL)
    feats = lax.all_gather(item_feat, "users", axis=0, tiled=True)

    ids = shard * clus + jnp.arange(clus, dtype=jnp.int32)
    taken = jnp.any(samples[None] == ids[:, None, None], axis=2)
    mask = jnp.repeat(jnp.where(taken, 0.0, NEG).astype(f32), BU, axis=1)
    pos_row = (pos_item - shard * rows).reshape(1, users)
    owner = (pos_item // rows).reshape(blocks, BU)

    in_specs = [
        pl.BlockSpec((rows, width + CL), lambda i: (0, 0)),
        pl.BlockSpec((STEP, width), lambda i: (i, 0)),
        pl.BlockSpec((clus, STEP), lambda i: (0, i)),
        pl.BlockSpec((1, STEP), lambda i: (0, i)),
    ]
    params = pltpu.CompilerParams(vmem_limit_bytes=48 << 20)
    table = pl.BlockSpec((blocks, BU), lambda i: (0, 0))
    lines = users // width
    lse, own_pos, below = pl.pallas_call(
        forward,
        grid=(steps,),
        in_specs=in_specs,
        out_specs=[table, table, pl.BlockSpec((lines, width), lambda i: (0, 0))],
        out_shape=[
            jax.ShapeDtypeStruct((blocks, BU), f32),
            jax.ShapeDtypeStruct((blocks, BU), f32),
            jax.ShapeDtypeStruct((lines, width), f32),
        ],
        compiler_params=params,
    )(items, user_emb, mask, pos_row)
    lses = spread(lse, "items", shards)
    grad, high, gap = pl.pallas_call(
        backward,
        grid=(steps,),
        in_specs=in_specs + [pl.BlockSpec((shards, blocks, BU), lambda i: (0, 0, 0)), table, table],
        out_specs=[
            pl.BlockSpec((STEP, width), lambda i: (i, 0)),
            pl.BlockSpec((rows, 2 * width), lambda i: (0, 0)),
            table,
        ],
        out_shape=[
            pltpu.HBM((users, width), f32),
            jax.ShapeDtypeStruct((rows, 2 * width), bf16),
            jax.ShapeDtypeStruct((blocks, BU), f32),
        ],
        scratch_shapes=[
            pltpu.VMEM((width, rows), bf16),
            pltpu.VMEM((blocks, BU), f32),
            pltpu.VMEM((blocks, BU), f32),
            pltpu.VMEM((rows, width), f32),
        ],
        compiler_params=params,
    )(items, user_emb, mask, pos_row, lses, own_pos, owner)

    user_grad = lax.psum_scatter(grad, "items", scatter_dimension=0, tiled=True)

    part = lax.dot_general(feats, high, (((0,), (0,)), ((), ())), preferred_element_type=f32)
    part = (part[:, :width] + part[:, width:]).astype(bf16)
    cut = part.shape[0] // group
    part, below = lax.optimization_barrier((part, below.astype(bf16)))
    part = lax.all_to_all(part.reshape(group, cut, width), "users", 0, 0)
    part = jnp.sum(part.astype(f32), axis=0).astype(bf16)
    both = spread(jnp.concatenate([part, below], axis=0), "items", shards)
    both = jnp.sum(both.astype(f32), axis=0)
    user_loss = gap.reshape(users) + both[cut:].reshape(users)
    part, user_loss = lax.optimization_barrier((both[:cut].astype(bf16), user_loss))
    weight_grad = spread(part, "users", group).reshape(group * cut, width).astype(f32)
    return user_loss, user_grad, weight_grad


def solution(mesh):
    return jax.shard_map(
        body,
        mesh=mesh,
        in_specs=(
            P("users", None),
            P("users", None),
            P("users"),
            P(("items", "users"), None),
            P(),
            P(("items", "users")),
        ),
        out_specs=(P("users"), P(("users", "items"), None), P()),
        check_vma=False,
    )
```

```python
import jax
import jax.numpy as jnp
from jax import lax
from jax.experimental import pallas as pl
from jax.experimental.pallas import tpu as pltpu
from jax.sharding import PartitionSpec as P

CL = 128
BU = 128
STEP = 1024
NEG = -1e30
FLOOR = -1e29
NT = (((1,), (1,)), ((), ()))
f32 = jnp.float32
bf16 = jnp.bfloat16


def spread(x, axis, n):
    return lax.all_to_all(jnp.broadcast_to(x[None], (n,) + x.shape), axis, 0, 0)


def logits_of(item_ref, user_ref, mask_ref):
    width = user_ref.shape[1]
    raw = lax.dot_general(item_ref[:, :width], user_ref[...], NT, preferred_element_type=f32)
    bias = item_ref[:, width:].astype(f32)
    raw = raw + jnp.concatenate([bias] * (STEP // CL), axis=1)
    parts = [raw[c * CL : (c + 1) * CL] + mask_ref[c : c + 1, :] for c in range(raw.shape[0] // CL)]
    return raw, jnp.concatenate(parts, axis=0)


def at_positive(raw, pos_ref):
    return lax.broadcasted_iota(jnp.int32, raw.shape, 0) == pos_ref[...]


def forward(item_ref, user_ref, mask_ref, pos_ref, stat_ref):
    step = pl.program_id(0)
    raw, kept = logits_of(item_ref, user_ref, mask_ref)
    here = (pos_ref[...] >= 0) & (pos_ref[...] < raw.shape[0])
    pos = jnp.sum(jnp.where(at_positive(raw, pos_ref), raw, 0.0), axis=0, keepdims=True)
    pos = jnp.where(here, pos, NEG)
    peak = jnp.maximum(jnp.maximum(jnp.max(kept, axis=0, keepdims=True), pos), FLOOR)
    total = jnp.sum(jnp.exp(kept - peak), axis=0, keepdims=True) + jnp.exp(pos - peak)
    lse = jnp.where(total > 0.0, peak + jnp.log(jnp.maximum(total, 1e-37)), NEG)
    blocks = stat_ref.shape[0] // 2
    for h in range(STEP // BU):
        row = step * (STEP // BU) + h
        stat_ref[pl.ds(row, 1), :] = lse[:, h * BU : (h + 1) * BU]
        stat_ref[pl.ds(blocks + row, 1), :] = pos[:, h * BU : (h + 1) * BU]


def backward(item_ref, user_ref, mask_ref, pos_ref, stats_ref, grad_ref, high_ref, loss_ref, item_t, total_ref, weight_ref, sums):
    step = pl.program_id(0)
    width = user_ref.shape[1]
    blocks = loss_ref.shape[0]

    @pl.when(step == 0)
    def _():
        lse = stats_ref[:, :blocks, :]
        peak = jnp.max(lse, axis=0)
        total = peak + jnp.log(jnp.sum(jnp.exp(lse - peak[None]), axis=0))
        pos = jnp.max(stats_ref[:, blocks:, :], axis=0)
        total_ref[...] = total
        loss_ref[...] = total - pos
        weight_ref[...] = jnp.exp(pos - total) - 1.0
        item_t[...] = item_ref[:, :width].astype(f32).T.astype(bf16)
        sums[...] = jnp.zeros_like(sums)

    def row_of(ref):
        rows = [ref[pl.ds(step * (STEP // BU) + h, 1), :] for h in range(STEP // BU)]
        return jnp.concatenate(rows, axis=1)

    raw, kept = logits_of(item_ref, user_ref, mask_ref)
    soft = jnp.exp(kept - row_of(total_ref))
    soft = soft + jnp.where(at_positive(raw, pos_ref), row_of(weight_ref), 0.0)
    soft = soft.astype(bf16)
    sums[...] += jnp.dot(soft, user_ref[...], preferred_element_type=f32)
    grad_ref[...] = jnp.dot(item_t[...], soft, preferred_element_type=f32).T

    @pl.when(step == pl.num_programs(0) - 1)
    def _():
        high = sums[...].astype(bf16)
        high_ref[:, :width] = high
        high_ref[:, width:] = (sums[...] - high.astype(f32)).astype(bf16)


def body(user_emb, samples, pos_item, item_feat, tower_w, item_bias):
    group, shards = lax.axis_size("users"), lax.axis_size("items")
    shard = lax.axis_index("items")
    own, width = item_feat.shape[0], tower_w.shape[1]
    rows = own * group
    clus = rows // CL
    users, blocks = user_emb.shape[0], samples.shape[0]
    steps = users // STEP

    feat, bias = lax.optimization_barrier((item_feat, jnp.broadcast_to(item_bias[:, None], (own, CL))))
    own_emb = jnp.dot(feat, tower_w, preferred_element_type=f32).astype(bf16)
    packed = jnp.concatenate([own_emb, bias], axis=1)
    items = spread(packed, "users", group).reshape(rows, width + CL)
    feats = lax.all_gather(item_feat, "users", axis=0, tiled=True)

    ids = shard * clus + jnp.arange(clus, dtype=jnp.int32)
    taken = jnp.any(samples[None] == ids[:, None, None], axis=2)
    mask = jnp.repeat(jnp.where(taken, 0.0, NEG).astype(f32), BU, axis=1)
    pos_row = (pos_item - shard * rows).reshape(1, users)

    in_specs = [
        pl.BlockSpec((rows, width + CL), lambda i: (0, 0)),
        pl.BlockSpec((STEP, width), lambda i: (i, 0)),
        pl.BlockSpec((clus, STEP), lambda i: (0, i)),
        pl.BlockSpec((1, STEP), lambda i: (0, i)),
    ]
    params = pltpu.CompilerParams(vmem_limit_bytes=48 << 20)
    stat = pl.pallas_call(
        forward,
        grid=(steps,),
        in_specs=in_specs,
        out_specs=pl.BlockSpec((2 * blocks, BU), lambda i: (0, 0)),
        out_shape=jax.ShapeDtypeStruct((2 * blocks, BU), f32),
        compiler_params=params,
    )(items, user_emb, mask, pos_row)
    stats = spread(stat, "items", shards)
    grad, high, loss = pl.pallas_call(
        backward,
        grid=(steps,),
        in_specs=in_specs + [pl.BlockSpec((shards, 2 * blocks, BU), lambda i: (0, 0, 0))],
        out_specs=[
            pl.BlockSpec((STEP, width), lambda i: (i, 0)),
            pl.BlockSpec((rows, 2 * width), lambda i: (0, 0)),
            pl.BlockSpec((blocks, BU), lambda i: (0, 0)),
        ],
        out_shape=[
            pltpu.HBM((users, width), f32),
            jax.ShapeDtypeStruct((rows, 2 * width), bf16),
            jax.ShapeDtypeStruct((blocks, BU), f32),
        ],
        scratch_shapes=[
            pltpu.VMEM((width, rows), bf16),
            pltpu.VMEM((blocks, BU), f32),
            pltpu.VMEM((blocks, BU), f32),
            pltpu.VMEM((rows, width), f32),
        ],
        compiler_params=params,
    )(items, user_emb, mask, pos_row, stats)

    user_grad = lax.psum_scatter(grad, "items", scatter_dimension=0, tiled=True)

    part = lax.dot_general(feats, high, (((0,), (0,)), ((), ())), preferred_element_type=f32)
    part = (part[:, :width] + part[:, width:]).astype(bf16)
    cut = part.shape[0] // group
    part = lax.all_to_all(part.reshape(group, cut, width), "users", 0, 0)
    part = jnp.sum(part.astype(f32), axis=0).astype(bf16)
    part = jnp.sum(spread(part, "items", shards).astype(f32), axis=0).astype(bf16)
    weight_grad = spread(part, "users", group).reshape(group * cut, width).astype(f32)
    return loss.reshape(users), user_grad, weight_grad


def solution(mesh):
    return jax.shard_map(
        body,
        mesh=mesh,
        in_specs=(
            P("users", None),
            P("users", None),
            P("users"),
            P(("items", "users"), None),
            P(),
            P(("items", "users")),
        ),
        out_specs=(P("users"), P(("users", "items"), None), P()),
        check_vma=False,
    )
```

```python
import functools

import jax
import jax.numpy as jnp
from jax import lax
from jax.experimental import pallas as pl
from jax.experimental.pallas import tpu as pltpu
from jax.sharding import PartitionSpec as P

CL = 128
BU = 128
STEP = 1024
NEG = -1e30
FLOOR = -1e29
NT = (((1,), (1,)), ((), ()))
f32 = jnp.float32
bf16 = jnp.bfloat16


def spread(x, axis, n):
    return lax.all_to_all(jnp.broadcast_to(x[None], (n,) + x.shape), axis, 0, 0)


def logits_of(item_ref, user_ref):
    width = user_ref.shape[1]
    raw = lax.dot_general(item_ref[:, :width], user_ref[...], NT, preferred_element_type=f32)
    bias = item_ref[:, width:].astype(f32)
    return raw + jnp.concatenate([bias] * (STEP // CL), axis=1)


def at_positive(raw, pos_ref):
    return lax.broadcasted_iota(jnp.int32, raw.shape, 0) == pos_ref[...]


def forward(item_ref, user_ref, mask_ref, pos_ref, stat_ref):
    step = pl.program_id(0)
    raw = logits_of(item_ref, user_ref)
    tiles = [slice(c * CL, (c + 1) * CL) for c in range(raw.shape[0] // CL)]
    here = (pos_ref[...] >= 0) & (pos_ref[...] < raw.shape[0])
    pos = jnp.sum(jnp.where(at_positive(raw, pos_ref), raw, 0.0), axis=0, keepdims=True)
    pos = jnp.where(here, pos, NEG)
    tops = [jnp.max(raw[t], axis=0, keepdims=True) + mask_ref[c : c + 1, :] for c, t in enumerate(tiles)]
    peak = functools.reduce(jnp.maximum, tops, jnp.maximum(pos, FLOOR))
    total = jnp.exp(pos - peak)
    for c, t in enumerate(tiles):
        part = jnp.sum(jnp.exp(raw[t] - peak), axis=0, keepdims=True)
        total = total + jnp.where(mask_ref[c : c + 1, :] == 0.0, part, 0.0)
    lse = jnp.where(total > 0.0, peak + jnp.log(jnp.maximum(total, 1e-37)), NEG)
    blocks = stat_ref.shape[0] // 2
    for h in range(STEP // BU):
        row = step * (STEP // BU) + h
        stat_ref[pl.ds(row, 1), :] = lse[:, h * BU : (h + 1) * BU]
        stat_ref[pl.ds(blocks + row, 1), :] = pos[:, h * BU : (h + 1) * BU]


def backward(item_ref, user_ref, mask_ref, pos_ref, stats_ref, grad_ref, high_ref, loss_ref, item_t, total_ref, weight_ref, sums):
    step = pl.program_id(0)
    width = user_ref.shape[1]
    blocks = loss_ref.shape[0]

    @pl.when(step == 0)
    def _():
        lse = stats_ref[:, :blocks, :]
        peak = jnp.max(lse, axis=0)
        total = peak + jnp.log(jnp.sum(jnp.exp(lse - peak[None]), axis=0))
        pos = jnp.max(stats_ref[:, blocks:, :], axis=0)
        total_ref[...] = total
        loss_ref[...] = total - pos
        weight_ref[...] = jnp.exp(pos - total) - 1.0
        item_t[...] = item_ref[:, :width].astype(f32).T.astype(bf16)
        sums[...] = jnp.zeros_like(sums)

    def row_of(ref):
        rows = [ref[pl.ds(step * (STEP // BU) + h, 1), :] for h in range(STEP // BU)]
        return jnp.concatenate(rows, axis=1)

    raw = logits_of(item_ref, user_ref)
    shift = row_of(total_ref)
    tiles = [raw[c * CL : (c + 1) * CL] + (mask_ref[c : c + 1, :] - shift) for c in range(raw.shape[0] // CL)]
    soft = jnp.exp(jnp.concatenate(tiles, axis=0))
    soft = soft + jnp.where(at_positive(raw, pos_ref), row_of(weight_ref), 0.0)
    soft = soft.astype(bf16)
    sums[...] += jnp.dot(soft, user_ref[...], preferred_element_type=f32)
    grad_ref[...] = jnp.dot(item_t[...], soft, preferred_element_type=f32).T

    @pl.when(step == pl.num_programs(0) - 1)
    def _():
        high = sums[...].astype(bf16)
        high_ref[:, :width] = high
        high_ref[:, width:] = (sums[...] - high.astype(f32)).astype(bf16)


def body(user_emb, samples, pos_item, item_feat, tower_w, item_bias):
    group, shards = lax.axis_size("users"), lax.axis_size("items")
    shard = lax.axis_index("items")
    own, width = item_feat.shape[0], tower_w.shape[1]
    rows = own * group
    clus = rows // CL
    users, blocks = user_emb.shape[0], samples.shape[0]
    steps = users // STEP

    feat, bias = lax.optimization_barrier((item_feat, jnp.broadcast_to(item_bias[:, None], (own, CL))))
    own_emb = jnp.dot(feat, tower_w, preferred_element_type=f32).astype(bf16)
    packed = jnp.concatenate([own_emb, bias], axis=1)
    items = spread(packed, "users", group).reshape(rows, width + CL)
    feats = lax.all_gather(item_feat, "users", axis=0, tiled=True)

    ids = shard * clus + jnp.arange(clus, dtype=jnp.int32)
    taken = jnp.any(samples[None] == ids[:, None, None], axis=2)
    mask = jnp.repeat(jnp.where(taken, 0.0, NEG).astype(f32), BU, axis=1)
    pos_row = (pos_item - shard * rows).reshape(1, users)

    in_specs = [
        pl.BlockSpec((rows, width + CL), lambda i: (0, 0)),
        pl.BlockSpec((STEP, width), lambda i: (i, 0)),
        pl.BlockSpec((clus, STEP), lambda i: (0, i)),
        pl.BlockSpec((1, STEP), lambda i: (0, i)),
    ]
    params = pltpu.CompilerParams(vmem_limit_bytes=48 << 20)
    stat = pl.pallas_call(
        forward,
        grid=(steps,),
        in_specs=in_specs,
        out_specs=pl.BlockSpec((2 * blocks, BU), lambda i: (0, 0)),
        out_shape=jax.ShapeDtypeStruct((2 * blocks, BU), f32),
        compiler_params=params,
    )(items, user_emb, mask, pos_row)
    stats = spread(stat, "items", shards)
    grad, high, loss = pl.pallas_call(
        backward,
        grid=(steps,),
        in_specs=in_specs + [pl.BlockSpec((shards, 2 * blocks, BU), lambda i: (0, 0, 0))],
        out_specs=[
            pl.BlockSpec((STEP, width), lambda i: (i, 0)),
            pl.BlockSpec((rows, 2 * width), lambda i: (0, 0)),
            pl.BlockSpec((blocks, BU), lambda i: (0, 0)),
        ],
        out_shape=[
            pltpu.HBM((users, width), f32),
            jax.ShapeDtypeStruct((rows, 2 * width), bf16),
            jax.ShapeDtypeStruct((blocks, BU), f32),
        ],
        scratch_shapes=[
            pltpu.VMEM((width, rows), bf16),
            pltpu.VMEM((blocks, BU), f32),
            pltpu.VMEM((blocks, BU), f32),
            pltpu.VMEM((rows, width), f32),
        ],
        compiler_params=params,
    )(items, user_emb, mask, pos_row, stats)

    user_grad = lax.psum_scatter(grad, "items", scatter_dimension=0, tiled=True)

    part = lax.dot_general(feats, high, (((0,), (0,)), ((), ())), preferred_element_type=f32)
    part = (part[:, :width] + part[:, width:]).astype(bf16)
    cut = part.shape[0] // group
    part = lax.all_to_all(part.reshape(group, cut, width), "users", 0, 0)
    part = jnp.sum(part.astype(f32), axis=0).astype(bf16)
    part = jnp.sum(spread(part, "items", shards).astype(f32), axis=0).astype(bf16)
    weight_grad = spread(part, "users", group).reshape(group * cut, width).astype(f32)
    return loss.reshape(users), user_grad, weight_grad


def solution(mesh):
    return jax.shard_map(
        body,
        mesh=mesh,
        in_specs=(
            P("users", None),
            P("users", None),
            P("users"),
            P(("items", "users"), None),
            P(),
            P(("items", "users")),
        ),
        out_specs=(P("users"), P(("users", "items"), None), P()),
        check_vma=False,
    )
```
